32 devices in a mesh: stream: 8 (over y, x, core), span: 4 (over z).
Axes of the slice: x: 2, y: 2, z: 4, core: 2. Of those that a mesh axis runs over, the one named last changes fastest.
Arguments:
- fluid_pos: float32 [64, 32, 3, 128], P('stream', 'span'), may hold values from 0 to 1
- fluid_vel: float32 [64, 32, 3, 128], P('stream', 'span'), may hold values from -6 to 6
- fluid_mass: float32 [64, 32, 128], P('stream', 'span'), may hold values from 0.5 to 2
- fluid_count: int32 [64, 32], P('stream', 'span'), may hold values from 64 to 128
- clump_center: float32 [16384, 3], P(('stream', 'span')), may hold values from 0 to 1
- clump_vel: float32 [16384, 3], P(('stream', 'span')), may hold values from -6 to 6
- clump_arm: float32 [16384, 3, 128], P(('stream', 'span')), may hold values from -1.8 to 1.8
- margin_device: int32 [16384, 2], P(('stream', 'span')), may hold values from 0 to 31, all different within a row; in each aligned block of 512 rows (0 to 511, 512 to 1023, ...) at most 64 rows name the same one
- margin_block: int32 [16384, 2], P(('stream', 'span')), may hold values from 0 to 63
- margin_offset: float32 [16384, 2, 3], P(('stream', 'span')), may hold values from 0 to 1
- contact_partner: int32 [16384], P(('stream', 'span')), may hold values from 0 to 1023
Outputs:
- fluid_density: float32 [64, 32, 128], P('stream', 'span')
- clump_load: float32 [6, 16384], P(None, ('stream', 'span'))
The draws below stay inside these ranges and needn't reach their ends.
Inputs may be any that keep to these rules, and one draw needn't show every extreme that they name: `margin_device`: among the 1024 margins of one device's clumps, at most 64 name any one device, and some device is named exactly 64 times; the two margins of a clump name different devices.
All inputs are finite; a program needn't handle non-finite values.
Results may differ from the reference program's by a relative error of at most 0.0001.
Values sent between devices are 32-bit elements; how exact they have to be, the bound alone decides.
A program may use at most 128 MiB of HBM per device.

```python
import math
import jax
import jax.numpy as jnp
import numpy as np
from jax import lax

FBX = 8
FBY = 8
PB = 128
SPH = 128
CL = 512
CAP = 64
NXB = 64
NYB = 32
CLUMPS = 16384
N_SPAN = 4
DEVICES = 32


def with_ends(entries, key, least, largest):
    spot = [jax.random.randint(jax.random.fold_in(key, axis), (), 0, length) for axis, length in enumerate(entries.shape)]
    main_axis = entries.shape.index(max(entries.shape))
    next_to = spot[:main_axis] + [(spot[main_axis] + 1) % entries.shape[main_axis]] + spot[main_axis + 1:]
    return entries.at[tuple(spot)].set(least).at[tuple(next_to)].set(largest)


def block_scale(own_key, shape, cuts, low, high):
    level, own = 1.0, jax.random.fold_in(own_key, 6)
    for position, blocks in cuts:
        heights = jnp.exp(jax.random.uniform(jax.random.fold_in(own, position), (blocks,), jnp.float32, low / len(cuts), high / len(cuts)))
        level = level * jnp.repeat(heights, shape[position] // blocks).reshape([-1 if axis == position else 1 for axis in range(len(shape))])
    return level


def deal_out(rng, own, number, rows, amount, top, limit, slope):
    sequence = jax.random.permutation(rng, amount)
    crowded, usual = load_shares(amount, rows * top, limit, slope, True), load_shares(amount, rows * top, limit, slope, False)
    places = jnp.arange(amount)

    def named(lengths, turn):
        used = int((lengths > 0).sum())
        fixed = max(1, used // 4)
        passed = fixed + (places - fixed + turn * (used - fixed)) % max(1, amount - fixed)
        return jnp.zeros((amount,), jnp.int32).at[sequence[jnp.where(places < fixed, places, passed)]].set(jnp.asarray(lengths, jnp.int32))

    lengths = jnp.where(number % 4 == 0, named(crowded, number // 4), named(usual, number - number // 4 - 1))
    mixed = jax.random.permutation(jax.random.fold_in(own, 3), amount)
    source_of, receiver = mixed[0:amount // 2 * 2:2], mixed[1:amount // 2 * 2:2]
    margin = jnp.minimum(lengths[source_of] - 1, limit - lengths[receiver]) // 2
    margin = jnp.where((source_of == sequence[0]) | (receiver == sequence[0]) | (lengths[receiver] == 0), 0, jnp.maximum(margin, 0))
    passed = jax.random.randint(jax.random.fold_in(own, 4), (amount // 2,), 0, 1 << 20) % (margin + 1)
    lengths = lengths.at[source_of].add(-passed).at[receiver].add(passed)
    members = jnp.searchsorted(jnp.cumsum(lengths), jnp.arange(rows * top), side="right").astype(jnp.int32)
    listing = members.reshape(top, rows).T
    listing = listing[jax.random.permutation(jax.random.fold_in(own, 1), rows)]
    turn = jax.random.randint(jax.random.fold_in(own, 2), (rows, 1), 0, top)
    return jnp.take_along_axis(listing, (jnp.arange(top)[None, :] + turn) % top, axis=1)


def load_shares(count, total, limit, slope, full):
    weights = [(1 << 20) // math.isqrt(rank ** slope) + 1 for rank in range(1, count + 1)]
    largest = limit if full else min(limit, max(-(-total // count), total * weights[0] // sum(weights)))
    least = 1 if total - largest >= count - 1 else 0
    counts, spare = [largest] + [least] * (count - 1), total - largest - least * (count - 1)
    while spare > 0:
        free = [i for i in range(1, count) if counts[i] < largest] or [i for i in range(1, count) if counts[i] < limit]
        mass, budget = sum([weights[i] for i in free]), spare
        for i in free:
            extra = min(limit - counts[i], max(1, budget * weights[i] // mass), spare)
            counts[i] = counts[i] + extra
            spare = spare - extra
    return np.array(counts)


def bell_draw(own_key, shape, spread, most, cuts=(), held_as=jnp.bfloat16):
    gain = block_scale(own_key, shape, cuts, -0.22, 0.18) if cuts else 1.0
    values = jax.random.normal(own_key, shape, jnp.float32) * spread * gain
    return jnp.minimum(jnp.maximum(values, -most), most).astype(held_as)


def setup_inputs(seed: int = 0) -> dict:
    seeds = jax.random.split(jax.random.key(seed), 12)
    fluid_pos = jnp.clip(1.0 * jax.random.uniform(seeds[0], (NXB, NYB, 3, PB), jnp.float32) ** block_scale(seeds[0], (NXB, NYB, 3, PB), ((0, 8), (1, 4)), -0.2, 0.2), 0.0, 1.0)
    fluid_vel = bell_draw(seeds[1], (NXB, NYB, 3, PB), 1.0, 6.0, ((0, 8), (1, 4)), jnp.float32)
    fluid_mass = jnp.clip(jnp.exp(math.log(2.0) - 1.3862944 * jax.random.uniform(seeds[2], (NXB, NYB, PB), jnp.float32) ** block_scale(seeds[2], (NXB, NYB, PB), ((0, 8), (1, 4)), -0.2, 0.2)), 0.5, 2.0)
    fluid_count = with_ends(jax.random.randint(seeds[3], (NXB, NYB), PB // 2, PB + 1), jax.random.fold_in(seeds[3], 1), PB // 2, PB).astype(jnp.int32)
    clump_center = jnp.clip(1.0 * jax.random.uniform(seeds[4], (CLUMPS, 3), jnp.float32) ** block_scale(seeds[4], (CLUMPS, 3), ((0, 32),), -0.2, 0.2), 0.0, 1.0)
    clump_vel = bell_draw(seeds[5], (CLUMPS, 3), 1.0, 6.0, ((0, 32),), jnp.float32)
    clump_arm = bell_draw(seeds[6], (CLUMPS, 3, SPH), 0.3, 1.8, ((0, 32),), jnp.float32)
    margin_device_keys = jax.random.split(jax.random.fold_in(seeds[7], 1), CLUMPS // CL)
    margin_device_turns = jax.random.permutation(jax.random.fold_in(seeds[7], 3), CLUMPS // CL)
    margin_device = jax.vmap(lambda own, number: deal_out(jax.random.fold_in(seeds[7], 2), own, number, CL, DEVICES, 2, CAP, 2))(margin_device_keys, margin_device_turns).reshape((CLUMPS, 2))
    margin_block = with_ends(jax.random.randint(seeds[8], (CLUMPS, 2), 0, FBX * FBY), jax.random.fold_in(seeds[8], 1), 0, (FBX * FBY) - 1).astype(jnp.int32)
    margin_offset = jnp.clip(1.0 * jax.random.uniform(seeds[9], (CLUMPS, 2, 3), jnp.float32) ** block_scale(seeds[9], (CLUMPS, 2, 3), ((0, 32),), -0.2, 0.2), 0.0, 1.0)
    contact_partner = with_ends(jax.random.randint(seeds[10], (CLUMPS,), 0, 2 * CL), jax.random.fold_in(seeds[10], 1), 0, (2 * CL) - 1).astype(jnp.int32)
    return dict(fluid_pos=fluid_pos, fluid_vel=fluid_vel, fluid_mass=fluid_mass, fluid_count=fluid_count, clump_center=clump_center, clump_vel=clump_vel, clump_arm=clump_arm, margin_device=margin_device, margin_block=margin_block, margin_offset=margin_offset, contact_partner=contact_partner)


H_SQ = 0.25
SIG_SQ = 0.5
DENS = 0.03125
DRAG = 0.002
STIFF = 0.005


def particle_mask(fluid_count, width):
    lanes = jnp.arange(width, dtype=jnp.int32)
    return (lanes[None, None, :] < fluid_count[..., None]).astype(jnp.float32)


def pair_sum(center, neigh, shift_x, shift_y):
    delta_x = center[:, 0, :, None] - neigh[:, 0, None, :] - shift_x
    delta_y = center[:, 1, :, None] - neigh[:, 1, None, :] - shift_y
    delta_z = center[:, 2, :, None] - neigh[:, 2, None, :]
    kernel = jnp.exp(-(delta_x * delta_x + delta_y * delta_y + delta_z * delta_z) / H_SQ)
    return jnp.sum(kernel * neigh[:, 3, None, :], axis=2)


def tile_force(pos, amp, offset, arm, velocity):
    spot = offset[:, None] + arm
    delta = pos[:, :, None] - spot[:, None, :]
    kernel = jnp.exp(-jnp.sum(delta * delta, axis=0) / H_SQ)
    acc = jnp.dot(amp, kernel, precision=lax.Precision.HIGHEST)
    return DRAG * (acc[:3] - velocity[:, None] * acc[3][None, :])


def contact_force(mine, other):
    delta = mine[:, :, None] - other[:, None, :]
    kernel = jnp.exp(-jnp.sum(delta * delta, axis=0) / SIG_SQ)
    pulled = jnp.dot(other, kernel.T, precision=lax.Precision.HIGHEST)
    return STIFF * (mine * jnp.sum(kernel, axis=1)[None, :] - pulled)


def reference(fluid_pos, fluid_vel, fluid_mass, fluid_count, clump_center, clump_vel, clump_arm, margin_device, margin_block, margin_offset, contact_partner):
    rows_x, rows_y, width = fluid_mass.shape
    live = particle_mask(fluid_count, width)
    packed = jnp.concatenate([fluid_pos, (live * fluid_mass)[:, :, None, :]], axis=2)
    padded = jnp.pad(packed, ((1, 1), (1, 1), (0, 0), (0, 0)))

    def one_row(row):
        center = lax.dynamic_index_in_dim(padded, row + 1, 0, keepdims=False)[1:-1]
        total = jnp.zeros((rows_y, width), jnp.float32)
        for step_x in (-1, 0, 1):
            line = lax.dynamic_index_in_dim(padded, row + 1 + step_x, 0, keepdims=False)
            for step_y in (-1, 0, 1):
                total = total + pair_sum(center, line[1 + step_y:1 + step_y + rows_y], float(step_x), float(step_y))
        return total

    sums = lax.map(one_row, jnp.arange(rows_x, dtype=jnp.int32))
    fluid_density = DENS * (fluid_mass + sums)
    weight = live * fluid_mass / fluid_density
    amp = jnp.concatenate([fluid_vel * weight[:, :, None, :], weight[:, :, None, :]], axis=2)
    pos_table = fluid_pos.reshape(rows_x * rows_y, 3, width)
    amp_table = amp.reshape(rows_x * rows_y, 4, width)
    global_x = (margin_device // N_SPAN) * FBX + margin_block // FBY
    global_y = (margin_device % N_SPAN) * FBY + margin_block % FBY
    flat_block = (global_x * rows_y + global_y).astype(jnp.int32)
    owner = jnp.arange(CLUMPS, dtype=jnp.int32) // CL
    partner = ((owner * CL + contact_partner) % CLUMPS).astype(jnp.int32)
    world = clump_center[:, :, None] + clump_arm

    def one_clump(item):
        blocks, offsets, arm, velocity, mine, partner_index = item
        force = tile_force(pos_table[blocks[0]], amp_table[blocks[0]], offsets[0], arm, velocity)
        force = force + tile_force(pos_table[blocks[1]], amp_table[blocks[1]], offsets[1], arm, velocity)
        force = force + contact_force(mine, world[partner_index])
        torque = jnp.cross(arm, force, axis=0)
        return jnp.concatenate([jnp.sum(force, axis=1), jnp.sum(torque, axis=1)])

    loads = lax.map(one_clump, (flat_block, margin_offset, clump_arm, clump_vel, world, partner), batch_size=64)
    return fluid_density, loads.T
```

```python
import functools

import jax
import jax.numpy as jnp
from jax import lax
from jax.experimental import pallas as pl
from jax.experimental.pallas import tpu as pltpu
from jax.sharding import PartitionSpec as P

INV_H = 4.0
INV_SIG = 2.0
DENS = 0.03125
DRAG = 0.002
STIFF = 0.005
AXES = ("stream", "span")
VMEM_BYTES = 58 * 1024 * 1024


def extended(cells, sides, width):
    for axis, dim in sides:
        count = lax.axis_size(axis)
        ends = count - 1
        head = lax.slice_in_dim(cells, 0, width, axis=dim)
        tail = lax.slice_in_dim(cells, cells.shape[dim] - width, cells.shape[dim], axis=dim)
        cells = jnp.concatenate(
            [
                lax.ppermute(tail, axis, [(i, (i + 1) % count) for i in range(ends)]),
                cells,
                lax.ppermute(head, axis, [((i + 1) % count, i) for i in range(ends)]),
            ],
            axis=dim,
        )
    return cells


def split(value):
    high = value.astype(jnp.bfloat16).astype(jnp.float32)
    rest = value - high
    mid = rest.astype(jnp.bfloat16).astype(jnp.float32)
    return high, mid, rest - mid


def near_stack(value):
    a, b, c = split(value)
    return jnp.concatenate([a, a, a, b, b, c], axis=0).astype(jnp.bfloat16)


def far_stack(value):
    a, b, c = split(value)
    return jnp.concatenate([a, b, c, a, b, a], axis=0).astype(jnp.bfloat16)


def near_rows(point, row):
    point = jnp.where(row < 3, point, 0.0)
    norm = jnp.sum(point * point, axis=0, keepdims=True)
    return jnp.where(row == 3, norm, jnp.where(row == 4, 1.0, point))


def far_rows(point, row, scale, extra):
    norm = jnp.sum(point * point, axis=0, keepdims=True)
    last = extra - scale * norm
    return jnp.where(row == 3, -scale, jnp.where(row == 4, last, (2.0 * scale) * point))


def column(row, x, y, z):
    return jnp.where(row == 0, x, jnp.where(row == 1, y, jnp.where(row == 2, z, 0.0)))


def exponents(near, far):
    return lax.dot_general(
        near, far, (((0,), (0,)), ((), ())), preferred_element_type=jnp.float32
    )


def gathered_sum(amp, kernel):
    both = lax.dot_general(
        amp, kernel, (((1,), (1,)), ((), ())), preferred_element_type=jnp.float32
    )
    return both[0:8] + both[8:16]


def amp_stack(value):
    high = value.astype(jnp.bfloat16).astype(jnp.float32)
    return jnp.concatenate([high, value - high], axis=0).astype(jnp.bfloat16)


def density_kernel(rows_x, rows_y, cells_ref, out_ref):
    row = lax.broadcasted_iota(jnp.int32, (8, 128), 0)

    def step(index, carry):
        bx = index // rows_y
        by = index % rows_y
        near = near_stack(near_rows(cells_ref[bx + 1, by + 1], row))
        total = jnp.zeros((128, 128), jnp.float32)
        for step_x in (-1, 0, 1):
            for step_y in (-1, 0, 1):
                cell = cells_ref[bx + 1 + step_x, by + 1 + step_y]
                point = jnp.where(
                    row < 3, cell + column(row, float(step_x), float(step_y), 0.0), 0.0
                )
                far = far_stack(far_rows(point, row, INV_H, cell[3:4]))
                total = total + jnp.exp(exponents(near, far))
        out_ref[pl.ds(index, 1), :] = jnp.sum(total.T, axis=0, keepdims=True)
        return carry

    lax.fori_loop(0, rows_x * rows_y, step, 0)


def contact_kernel(clumps, batch, partner_ref, center_ref, near_ref, out_ref):
    row = lax.broadcasted_iota(jnp.int32, (8, 128), 0)

    def step(index, carry):
        for k in range(batch):
            c = index * batch + k
            p = partner_ref[c]
            shift = column(
                row,
                center_ref[3 * p] - center_ref[3 * c],
                center_ref[3 * p + 1] - center_ref[3 * c + 1],
                center_ref[3 * p + 2] - center_ref[3 * c + 2],
            )
            near = near_stack(near_ref[c])
            point = jnp.where(row < 3, near_ref[p] + shift, 0.0)
            far = far_stack(far_rows(point, row, INV_SIG, 0.0))
            kernel = jnp.exp(exponents(near, far)).astype(jnp.bfloat16)
            amp = amp_stack(jnp.where(row == 3, 1.0, point))
            out_ref[c] = gathered_sum(amp, kernel)
        return carry

    lax.fori_loop(0, clumps // batch, step, 0)


def fluid_kernel(clumps, batch, block_ref, offset_ref, near_ref, table_ref, out_ref):
    row = lax.broadcasted_iota(jnp.int32, (8, 128), 0)

    def step(index, carry):
        for k in range(batch):
            c = index * batch + k
            near = near_stack(near_ref[c])
            fars, amps = [], []
            for m in range(2):
                e = 2 * c + m
                cell = table_ref[block_ref[e]]
                shift = column(
                    row, offset_ref[3 * e], offset_ref[3 * e + 1], offset_ref[3 * e + 2]
                )
                point = jnp.where(row < 3, cell - shift, 0.0)
                fars.append(far_stack(far_rows(point, row, INV_H, 0.0)))
                amps.append(amp_stack(cell))
            far = jnp.concatenate(fars, axis=1)
            amp = jnp.concatenate(amps, axis=1)
            kernel = jnp.exp(exponents(near, far)).astype(jnp.bfloat16)
            out_ref[c] = gathered_sum(amp, kernel)
        return carry

    lax.fori_loop(0, clumps // batch, step, 0)


def call(kernel, shape, scalars, arrays, tiles):
    smem = pl.BlockSpec(memory_space=pltpu.SMEM)
    vmem = pl.BlockSpec(memory_space=pltpu.VMEM)
    return pl.pallas_call(
        kernel,
        out_shape=jax.ShapeDtypeStruct(shape, jnp.float32),
        in_specs=[smem] * len(scalars) + [vmem] * len(arrays),
        out_specs=vmem,
        compiler_params=pltpu.CompilerParams(vmem_limit_bytes=VMEM_BYTES),
        cost_estimate=pl.CostEstimate(
            flops=tiles * 128 * 128 * 128,
            bytes_accessed=4 * sum(a.size for a in arrays),
            transcendentals=tiles * 128 * 128,
        ),
    )(*scalars, *arrays)


def body(
    fluid_pos,
    fluid_vel,
    fluid_mass,
    fluid_count,
    clump_center,
    clump_vel,
    clump_arm,
    margin_device,
    margin_block,
    margin_offset,
    contact_partner,
):
    rows_x, rows_y, width = fluid_mass.shape
    cells = rows_x * rows_y
    clumps = clump_arm.shape[0]
    spheres = clump_arm.shape[2]
    devices = lax.axis_size(AXES)
    back = [(i, (i + devices - 1) % devices) for i in range(devices)]

    lanes = jnp.arange(width, dtype=jnp.int32)
    live = (lanes[None, None, :] < fluid_count[..., None]).astype(jnp.float32)
    live_mass = live * fluid_mass
    centered = fluid_pos - 0.5
    packed = jnp.concatenate([centered, live_mass[:, :, None, :]], axis=2)
    padded = extended(packed, (("stream", 0), ("span", 1)), 1)
    mass = padded[:, :, 3:4]
    log_mass = jnp.where(mass > 0, jnp.log(jnp.maximum(mass, 1e-30)), -1e30)
    padded = jnp.concatenate(
        [padded[:, :, 0:3], log_mass, jnp.zeros(padded.shape[:2] + (4, width), jnp.float32)],
        axis=2,
    )
    sums = call(
        functools.partial(density_kernel, rows_x, rows_y),
        (cells, width),
        (),
        (padded,),
        9 * cells,
    )
    fluid_density = DENS * (fluid_mass + sums.reshape(rows_x, rows_y, width))
    weight = (live_mass / fluid_density)[:, :, None, :]
    table = jnp.concatenate(
        [centered, jnp.zeros_like(weight), fluid_vel * weight, weight], axis=2
    ).reshape(cells, 8, width)
    table = lax.all_gather(table, AXES, axis=0, tiled=True)

    center_next = lax.ppermute(clump_center, AXES, back)
    arm_next = lax.ppermute(clump_arm, AXES, back)
    centers = jnp.concatenate([clump_center, center_next], axis=0).reshape(-1)
    arms = jnp.concatenate([clump_arm, arm_next], axis=0)
    near = jnp.concatenate(
        [
            arms,
            jnp.sum(arms * arms, axis=1, keepdims=True),
            jnp.ones((2 * clumps, 1, spheres), jnp.float32),
            jnp.zeros((2 * clumps, 3, spheres), jnp.float32),
        ],
        axis=1,
    )
    batch = 4
    pulled = call(
        functools.partial(contact_kernel, clumps, batch),
        (clumps, 8, spheres),
        (contact_partner, centers),
        (near,),
        clumps,
    )
    carried = call(
        functools.partial(fluid_kernel, clumps, batch),
        (clumps, 8, spheres),
        (
            (margin_device * cells + margin_block).reshape(-1),
            (margin_offset - 0.5).reshape(-1),
        ),
        (near[:clumps], table),
        2 * clumps,
    )
    force = DRAG * (carried[:, 4:7] - clump_vel[:, :, None] * carried[:, 7:8]) + STIFF * (
        clump_arm * pulled[:, 3:4] - pulled[:, 0:3]
    )
    load = jnp.concatenate(
        [jnp.sum(force, axis=2), jnp.sum(jnp.cross(clump_arm, force, axis=1), axis=2)], axis=1
    )
    return (fluid_density, load.T)


def solution(mesh):
    in_specs = (
        P("stream", "span", None, None),
        P("stream", "span", None, None),
        P("stream", "span", None),
        P("stream", "span"),
        P(AXES, None),
        P(AXES, None),
        P(AXES, None, None),
        P(AXES, None),
        P(AXES, None),
        P(AXES, None, None),
        P(AXES),
    )
    out_specs = (P("stream", "span", None), P(None, AXES))
    return jax.shard_map(body, mesh=mesh, in_specs=in_specs, out_specs=out_specs, check_vma=False)
```

```python
import functools

import jax
import jax.numpy as jnp
from jax import lax
from jax.experimental import pallas as pl
from jax.experimental.pallas import tpu as pltpu
from jax.sharding import PartitionSpec as P

INV_H = 4.0
INV_SIG = 2.0
DENS = 0.03125
DRAG = 0.002
STIFF = 0.005
AXES = ("stream", "span")
VMEM_BYTES = 58 * 1024 * 1024


def extended(cells, sides, width):
    for axis, dim in sides:
        count = lax.axis_size(axis)
        ends = count - 1
        head = lax.slice_in_dim(cells, 0, width, axis=dim)
        tail = lax.slice_in_dim(cells, cells.shape[dim] - width, cells.shape[dim], axis=dim)
        cells = jnp.concatenate(
            [
                lax.ppermute(tail, axis, [(i, (i + 1) % count) for i in range(ends)]),
                cells,
                lax.ppermute(head, axis, [((i + 1) % count, i) for i in range(ends)]),
            ],
            axis=dim,
        )
    return cells


def split(value):
    high = value.astype(jnp.bfloat16).astype(jnp.float32)
    rest = value - high
    mid = rest.astype(jnp.bfloat16).astype(jnp.float32)
    return high, mid, rest - mid


def near_stack(value):
    a, b, c = split(value)
    return turned(jnp.concatenate([a, a, a, b, b, c], axis=0))


def far_stack(value):
    a, b, c = split(value)
    return jnp.concatenate([a, b, c, a, b, a], axis=0).astype(jnp.bfloat16)


def near_rows(point, row):
    point = jnp.where(row < 3, point, 0.0)
    norm = jnp.sum(point * point, axis=0, keepdims=True)
    return jnp.where(row == 3, norm, jnp.where(row == 4, 1.0, point))


def far_rows(point, row, scale, extra):
    norm = jnp.sum(point * point, axis=0, keepdims=True)
    last = extra - scale * norm
    return jnp.where(row == 3, -scale, jnp.where(row == 4, last, (2.0 * scale) * point))


def column(row, x, y, z):
    return jnp.where(row == 0, x, jnp.where(row == 1, y, jnp.where(row == 2, z, 0.0)))


def turned(stack):
    return stack.T.astype(jnp.bfloat16)


def exponents(near, far):
    return jnp.dot(near, far, preferred_element_type=jnp.float32)


def gathered_sum(amp, kernel):
    both = lax.dot_general(
        amp, kernel, (((1,), (1,)), ((), ())), preferred_element_type=jnp.float32
    )
    return both[0:8] + both[8:16]


def amp_stack(value):
    high = value.astype(jnp.bfloat16).astype(jnp.float32)
    return jnp.concatenate([high, value - high], axis=0).astype(jnp.bfloat16)


def density_kernel(rows_x, rows_y, cells_ref, out_ref):
    row = lax.broadcasted_iota(jnp.int32, (8, 128), 0)
    steps = [(x, y) for x in (-1, 0, 1) for y in (-1, 0, 1)]

    def step(index, carry):
        bx = index // rows_y
        by = index % rows_y
        near = near_stack(near_rows(cells_ref[bx + 1, by + 1], row))
        fars = []
        for x, y in steps:
            cell = cells_ref[bx + 1 + x, by + 1 + y]
            point = jnp.where(row < 3, cell + column(row, float(x), float(y), 0.0), 0.0)
            fars.append(far_stack(far_rows(point, row, INV_H, cell[3:4])))
        total = jnp.zeros((128, 128), jnp.float32)
        for k in range(0, len(fars), 2):
            far = jnp.concatenate(fars[k : k + 2], axis=1)
            kernel = jnp.exp(exponents(near, far))
            for part in range(0, kernel.shape[1], 128):
                total = total + kernel[:, part : part + 128]
        out_ref[pl.ds(index, 1), :] = jnp.sum(total.T, axis=0, keepdims=True)
        return carry

    lax.fori_loop(0, rows_x * rows_y, step, 0)


def contact_kernel(clumps, batch, partner_ref, center_ref, near_ref, out_ref):
    row = lax.broadcasted_iota(jnp.int32, (8, 128), 0)

    def step(index, carry):
        nears, points = [], []
        for k in range(batch):
            c = index * batch + k
            p = partner_ref[c]
            shift = column(
                row,
                center_ref[3 * p] - center_ref[3 * c],
                center_ref[3 * p + 1] - center_ref[3 * c + 1],
                center_ref[3 * p + 2] - center_ref[3 * c + 2],
            )
            nears.append(near_ref[c])
            points.append(jnp.where(row < 3, near_ref[p] + shift, 0.0))
        nears = [near_stack(near) for near in nears]
        fars = [far_stack(far_rows(point, row, INV_SIG, 0.0)) for point in points]
        amps = [amp_stack(jnp.where(row == 3, 1.0, point)) for point in points]
        logs = [exponents(near, far) for near, far in zip(nears, fars)]
        kernels = [jnp.exp(log).astype(jnp.bfloat16) for log in logs]
        sums = [gathered_sum(amp, kernel) for amp, kernel in zip(amps, kernels)]
        for k in range(batch):
            out_ref[index * batch + k] = sums[k]
        return carry

    lax.fori_loop(0, clumps // batch, step, 0)


def fluid_kernel(
    clumps, batch, block_ref, offset_ref, near_ref, weight_ref, hbm_ref, out_ref, table_ref, sem
):
    row = lax.broadcasted_iota(jnp.int32, (8, 128), 0)
    filled = hbm_ref.shape[0]
    fetch = pltpu.make_async_copy(hbm_ref, table_ref.at[pl.ds(0, filled)], sem)
    fetch.start()
    table_ref[filled:] = jnp.zeros((8, 128), jnp.float32)
    fetch.wait()

    def step(index, carry):
        nears, cells, weights, shifts = [], [], [], []
        for k in range(batch):
            c = index * batch + k
            nears.append(near_ref[c])
            for m in range(2):
                e = 2 * c + m
                block = block_ref[e]
                cells.append(table_ref[pl.ds(6 * block, 8), :])
                weights.append(weight_ref[pl.ds(block, 1), :])
                shifts.append(
                    column(row, offset_ref[3 * e], offset_ref[3 * e + 1], offset_ref[3 * e + 2])
                )
        nears = [near_stack(near) for near in nears]
        points = [jnp.where(row < 3, cell - shift, 0.0) for cell, shift in zip(cells, shifts)]
        fars = [far_stack(far_rows(point, row, INV_H, 0.0)) for point in points]
        amps = [
            amp_stack(jnp.where(row == 6, 1.0, jnp.where(row == 7, 0.0, cell)) * weight)
            for cell, weight in zip(cells, weights)
        ]
        logs = [
            exponents(near, jnp.concatenate(fars[2 * k : 2 * k + 2], axis=1))
            for k, near in enumerate(nears)
        ]
        kernels = [jnp.exp(log).astype(jnp.bfloat16) for log in logs]
        sums = [
            gathered_sum(jnp.concatenate(amps[2 * k : 2 * k + 2], axis=1), kernel)
            for k, kernel in enumerate(kernels)
        ]
        for k in range(batch):
            out_ref[index * batch + k] = sums[k]
        return carry

    lax.fori_loop(0, clumps // batch, step, 0)


def call(kernel, shape, scalars, arrays, tiles, held=(), scratch=()):
    smem = pl.BlockSpec(memory_space=pltpu.SMEM)
    vmem = pl.BlockSpec(memory_space=pltpu.VMEM)
    return pl.pallas_call(
        kernel,
        out_shape=jax.ShapeDtypeStruct(shape, jnp.float32),
        in_specs=[smem] * len(scalars) + [vmem] * len(arrays)
        + [pl.BlockSpec(memory_space=pl.ANY)] * len(held),
        out_specs=vmem,
        scratch_shapes=list(scratch),
        compiler_params=pltpu.CompilerParams(vmem_limit_bytes=VMEM_BYTES),
        cost_estimate=pl.CostEstimate(
            flops=tiles * 128 * 128 * 128 * 24,
            bytes_accessed=4 * sum(a.size for a in arrays),
            transcendentals=tiles * 128 * 128,
        ),
    )(*scalars, *arrays, *held)


def body(
    fluid_pos,
    fluid_vel,
    fluid_mass,
    fluid_count,
    clump_center,
    clump_vel,
    clump_arm,
    margin_device,
    margin_block,
    margin_offset,
    contact_partner,
):
    rows_x, rows_y, width = fluid_mass.shape
    cells = rows_x * rows_y
    clumps = clump_arm.shape[0]
    spheres = clump_arm.shape[2]
    devices = lax.axis_size(AXES)
    back = [(i, (i + devices - 1) % devices) for i in range(devices)]

    lanes = jnp.arange(width, dtype=jnp.int32)
    live = (lanes[None, None, :] < fluid_count[..., None]).astype(jnp.float32)
    live_mass = live * fluid_mass
    centered = fluid_pos - 0.5
    table = jnp.concatenate([centered, fluid_vel], axis=2).reshape(cells * 6, width)
    table = lax.all_gather(table, AXES, axis=0, tiled=True)
    packed = jnp.concatenate([centered, live_mass[:, :, None, :]], axis=2)
    padded = extended(packed, (("stream", 0), ("span", 1)), 1)
    mass = padded[:, :, 3:4]
    log_mass = jnp.where(mass > 0, jnp.log(jnp.maximum(mass, 1e-30)), -1e30)
    padded = jnp.concatenate(
        [padded[:, :, 0:3], log_mass, jnp.zeros(padded.shape[:2] + (4, width), jnp.float32)],
        axis=2,
    )
    sums = call(
        functools.partial(density_kernel, rows_x, rows_y),
        (cells, width),
        (),
        (padded,),
        9 * cells,
    )
    fluid_density = DENS * (fluid_mass + sums.reshape(rows_x, rows_y, width))
    weights = lax.all_gather(
        (live_mass / fluid_density).reshape(cells, width), AXES, axis=0, tiled=True
    )

    center_next = lax.ppermute(clump_center, AXES, back)
    arm_next = lax.ppermute(clump_arm, AXES, back)
    centers = jnp.concatenate([clump_center, center_next], axis=0).reshape(-1)
    arms = jnp.concatenate([clump_arm, arm_next], axis=0)
    near = jnp.concatenate(
        [
            arms,
            jnp.sum(arms * arms, axis=1, keepdims=True),
            jnp.ones((2 * clumps, 1, spheres), jnp.float32),
            jnp.zeros((2 * clumps, 3, spheres), jnp.float32),
        ],
        axis=1,
    )
    batch = 4
    pulled = call(
        functools.partial(contact_kernel, clumps, batch),
        (clumps, 8, spheres),
        (contact_partner, centers),
        (near,),
        clumps,
    )
    carried = call(
        functools.partial(fluid_kernel, clumps, batch),
        (clumps, 8, spheres),
        (
            (margin_device * cells + margin_block).reshape(-1),
            (margin_offset - 0.5).reshape(-1),
        ),
        (near[:clumps], weights),
        2 * clumps,
        (table,),
        (
            pltpu.VMEM((table.shape[0] + 8, width), jnp.float32),
            pltpu.SemaphoreType.DMA,
        ),
    )
    force = DRAG * (carried[:, 3:6] - clump_vel[:, :, None] * carried[:, 6:7]) + STIFF * (
        clump_arm * pulled[:, 3:4] - pulled[:, 0:3]
    )
    load = jnp.concatenate(
        [jnp.sum(force, axis=2), jnp.sum(jnp.cross(clump_arm, force, axis=1), axis=2)], axis=1
    )
    return (fluid_density, load.T)


def solution(mesh):
    in_specs = (
        P("stream", "span", None, None),
        P("stream", "span", None, None),
        P("stream", "span", None),
        P("stream", "span"),
        P(AXES, None),
        P(AXES, None),
        P(AXES, None, None),
        P(AXES, None),
        P(AXES, None),
        P(AXES, None, None),
        P(AXES),
    )
    out_specs = (P("stream", "span", None), P(None, AXES))
    return jax.shard_map(body, mesh=mesh, in_specs=in_specs, out_specs=out_specs, check_vma=False)
```

```python
import functools

import jax
import jax.numpy as jnp
from jax import lax
from jax.experimental import pallas as pl
from jax.experimental.pallas import tpu as pltpu
from jax.sharding import PartitionSpec as P

INV_H = 4.0
INV_SIG = 2.0
DENS = 0.03125
DRAG = 0.002
STIFF = 0.005
AXES = ("stream", "span")
VMEM_BYTES = 58 * 1024 * 1024


def extended(cells, sides, width):
    for axis, dim in sides:
        count = lax.axis_size(axis)
        ends = count - 1
        head = lax.slice_in_dim(cells, 0, width, axis=dim)
        tail = lax.slice_in_dim(cells, cells.shape[dim] - width, cells.shape[dim], axis=dim)
        cells = jnp.concatenate(
            [
                lax.ppermute(tail, axis, [(i, (i + 1) % count) for i in range(ends)]),
                cells,
                lax.ppermute(head, axis, [((i + 1) % count, i) for i in range(ends)]),
            ],
            axis=dim,
        )
    return cells


def rounded(value):
    return value.astype(jnp.bfloat16).astype(jnp.float32)


def near_stack(point, row):
    point = jnp.where(row < 3, point, jnp.where(row == 3, 1.0, 0.0))
    high = rounded(point)
    low = jnp.where(row == 3, 1.0, point - high)
    return [high + pltpu.roll(high, 4, 0), low]


def far_stack(point, row, scale, extra):
    last = extra - scale * jnp.sum(point * point, axis=0, keepdims=True)
    value = jnp.where(row == 3, last, (2.0 * scale) * point)
    high = rounded(value)
    mid = rounded(value - high)
    third = jnp.where(row == 3, value - high - mid, high)
    return jnp.concatenate([high + pltpu.roll(mid, 4, 0), third], axis=0).astype(jnp.bfloat16)


def placed(fars, at, count):
    far = fars[0] if len(fars) == 1 else jnp.concatenate(fars, axis=1)
    width = far.shape[1]
    parts = [far]
    if at:
        parts = [jnp.zeros((16 * at, width), jnp.bfloat16)] + parts
    if at < count - 1:
        parts = parts + [jnp.zeros((16 * (count - 1 - at), width), jnp.bfloat16)]
    return jnp.concatenate(parts, axis=0)


def turned(stacks):
    return jnp.concatenate(stacks, axis=0).T.astype(jnp.bfloat16)


def column(row, x, y, z):
    return jnp.where(row == 0, x, jnp.where(row == 1, y, jnp.where(row == 2, z, 0.0)))


def exponents(near, far):
    return jnp.dot(near, far, preferred_element_type=jnp.float32)


def gathered_sum(amp, kernel):
    both = lax.dot_general(
        amp, kernel, (((1,), (1,)), ((), ())), preferred_element_type=jnp.float32
    )
    return both[0:8] + both[8:16]


def amp_stack(value):
    high = value.astype(jnp.bfloat16).astype(jnp.float32)
    return jnp.concatenate([high, value - high], axis=0).astype(jnp.bfloat16)


def density_kernel(rows_x, rows_y, batch, cells_ref, out_ref):
    row = lax.broadcasted_iota(jnp.int32, (8, 128), 0)
    steps = [(x, y) for x in (-1, 0, 1) for y in (-1, 0, 1)]

    def step(index, carry):
        cells, norms, stacks = [], [], []
        for k in range(batch):
            cell = index * batch + k
            cells.append((cell // rows_y, cell % rows_y))
            center = cells_ref[cells[k][0] + 1, cells[k][1] + 1]
            stacks += near_stack(center, row)
            norms.append(jnp.sum(jnp.where(row < 3, center * center, 0.0), axis=0, keepdims=True))
        near = turned(stacks)
        sums = []
        for k, (bx, by) in enumerate(cells):
            fars = []
            for x, y in steps:
                cell = cells_ref[bx + 1 + x, by + 1 + y]
                point = jnp.where(row < 3, cell + column(row, float(x), float(y), 0.0), 0.0)
                fars.append(far_stack(point, row, INV_H, cell[3:4]))
            total = None
            for first in range(0, len(fars), 2):
                kernel = jnp.exp(exponents(near, placed(fars[first : first + 2], k, batch)))
                for part in range(0, kernel.shape[1], 128):
                    piece = kernel[:, part : part + 128]
                    total = piece if total is None else total + piece
            sums.append(jnp.sum(total.T, axis=0, keepdims=True) * jnp.exp(-INV_H * norms[k]))
        for k in range(batch):
            out_ref[pl.ds(index * batch + k, 1), :] = sums[k]
        return carry

    lax.fori_loop(0, rows_x * rows_y // batch, step, 0)


def contact_kernel(clumps, batch, partner_ref, center_ref, near_ref, out_ref):
    row = lax.broadcasted_iota(jnp.int32, (8, 128), 0)

    def step(index, carry):
        nears, points = [], []
        for k in range(batch):
            c = index * batch + k
            p = partner_ref[c]
            shift = column(
                row,
                center_ref[3 * p] - center_ref[3 * c],
                center_ref[3 * p + 1] - center_ref[3 * c + 1],
                center_ref[3 * p + 2] - center_ref[3 * c + 2],
            )
            nears.append(near_ref[c])
            points.append(jnp.where(row < 3, near_ref[p] + shift, 0.0))
        turn = turned([part for near in nears for part in near_stack(near, row)])
        fars = [far_stack(point, row, INV_SIG, 0.0) for point in points]
        amps = [amp_stack(jnp.where(row == 3, 1.0, point)) for point in points]
        sums = []
        for k in range(batch):
            log = exponents(turn, placed(fars[k : k + 1], k, batch))
            total = gathered_sum(amps[k], jnp.exp(log).astype(jnp.bfloat16))
            sums.append(total * jnp.exp(-INV_SIG * nears[k][3:4]))
        for k in range(batch):
            out_ref[index * batch + k] = sums[k]
        return carry

    lax.fori_loop(0, clumps // batch, step, 0)


def fluid_kernel(
    clumps, batch, block_ref, offset_ref, near_ref, weight_ref, hbm_ref, out_ref, table_ref, sem
):
    row = lax.broadcasted_iota(jnp.int32, (8, 128), 0)
    filled = hbm_ref.shape[0]
    fetch = pltpu.make_async_copy(hbm_ref, table_ref.at[pl.ds(0, filled)], sem)
    fetch.start()
    table_ref[filled:] = jnp.zeros((8, 128), jnp.float32)
    fetch.wait()

    def step(index, carry):
        nears, cells, weights, shifts = [], [], [], []
        for k in range(batch):
            c = index * batch + k
            nears.append(near_ref[c])
            for m in range(2):
                e = 2 * c + m
                block = block_ref[e]
                cells.append(table_ref[pl.ds(6 * block, 8), :])
                weights.append(weight_ref[pl.ds(block, 1), :])
                shifts.append(
                    column(row, offset_ref[3 * e], offset_ref[3 * e + 1], offset_ref[3 * e + 2])
                )
        turn = turned([part for near in nears for part in near_stack(near, row)])
        points = [jnp.where(row < 3, cell - shift, 0.0) for cell, shift in zip(cells, shifts)]
        fars = [far_stack(point, row, INV_H, 0.0) for point in points]
        amps = [
            amp_stack(jnp.where(row == 6, 1.0, jnp.where(row == 7, 0.0, cell)) * weight)
            for cell, weight in zip(cells, weights)
        ]
        sums = []
        for k in range(batch):
            log = exponents(turn, placed(fars[2 * k : 2 * k + 2], k, batch))
            amp = jnp.concatenate(amps[2 * k : 2 * k + 2], axis=1)
            total = gathered_sum(amp, jnp.exp(log).astype(jnp.bfloat16))
            sums.append(total * jnp.exp(-INV_H * nears[k][3:4]))
        for k in range(batch):
            out_ref[index * batch + k] = sums[k]
        return carry

    lax.fori_loop(0, clumps // batch, step, 0)


def call(kernel, shape, scalars, arrays, tiles, held=(), scratch=()):
    smem = pl.BlockSpec(memory_space=pltpu.SMEM)
    vmem = pl.BlockSpec(memory_space=pltpu.VMEM)
    return pl.pallas_call(
        kernel,
        out_shape=jax.ShapeDtypeStruct(shape, jnp.float32),
        in_specs=[smem] * len(scalars) + [vmem] * len(arrays)
        + [pl.BlockSpec(memory_space=pl.ANY)] * len(held),
        out_specs=vmem,
        scratch_shapes=list(scratch),
        compiler_params=pltpu.CompilerParams(vmem_limit_bytes=VMEM_BYTES),
        cost_estimate=pl.CostEstimate(
            flops=tiles * 128,
            bytes_accessed=128 * tiles,
            transcendentals=tiles * 128,
        ),
    )(*scalars, *arrays, *held)


def body(
    fluid_pos,
    fluid_vel,
    fluid_mass,
    fluid_count,
    clump_center,
    clump_vel,
    clump_arm,
    margin_device,
    margin_block,
    margin_offset,
    contact_partner,
):
    rows_x, rows_y, width = fluid_mass.shape
    cells = rows_x * rows_y
    clumps = clump_arm.shape[0]
    spheres = clump_arm.shape[2]
    devices = lax.axis_size(AXES)
    back = [(i, (i + devices - 1) % devices) for i in range(devices)]

    lanes = jnp.arange(width, dtype=jnp.int32)
    live = (lanes[None, None, :] < fluid_count[..., None]).astype(jnp.float32)
    live_mass = live * fluid_mass
    centered = fluid_pos - 0.5
    table = jnp.concatenate([centered, fluid_vel], axis=2).reshape(cells * 6, width)
    table = lax.all_gather(table, AXES, axis=0, tiled=True)
    packed = jnp.concatenate([centered, live_mass[:, :, None, :]], axis=2)
    padded = extended(packed, (("stream", 0), ("span", 1)), 1)
    mass = padded[:, :, 3:4]
    log_mass = jnp.where(mass > 0, jnp.log(jnp.maximum(mass, 1e-30)), -1e30)
    padded = jnp.concatenate(
        [padded[:, :, 0:3], log_mass, jnp.zeros(padded.shape[:2] + (4, width), jnp.float32)],
        axis=2,
    )
    sums = call(
        functools.partial(density_kernel, rows_x, rows_y, 4),
        (cells, width),
        (),
        (padded,),
        9 * cells,
    )
    fluid_density = DENS * (fluid_mass + sums.reshape(rows_x, rows_y, width))
    weights = (live_mass / fluid_density).reshape(cells, width)
    weights, table = lax.optimization_barrier((weights, table))
    weights = lax.all_gather(weights, "span", axis=0, tiled=True)
    weights = lax.all_gather(weights, "stream", axis=0, tiled=True)

    center_next = lax.ppermute(clump_center, AXES, back)
    arm_next = lax.ppermute(clump_arm, AXES, back)
    centers = jnp.concatenate([clump_center, center_next], axis=0).reshape(-1)
    arms = jnp.concatenate([clump_arm, arm_next], axis=0)
    near = jnp.concatenate(
        [
            arms,
            jnp.sum(arms * arms, axis=1, keepdims=True),
            jnp.ones((2 * clumps, 1, spheres), jnp.float32),
            jnp.zeros((2 * clumps, 3, spheres), jnp.float32),
        ],
        axis=1,
    )
    batch = 8
    pulled = call(
        functools.partial(contact_kernel, clumps, batch),
        (clumps, 8, spheres),
        (contact_partner, centers),
        (near,),
        clumps,
    )
    carried = call(
        functools.partial(fluid_kernel, clumps, batch),
        (clumps, 8, spheres),
        (
            (margin_device * cells + margin_block).reshape(-1),
            (margin_offset - 0.5).reshape(-1),
        ),
        (near[:clumps], weights),
        2 * clumps,
        (table,),
        (
            pltpu.VMEM((table.shape[0] + 8, width), jnp.float32),
            pltpu.SemaphoreType.DMA,
        ),
    )
    force = DRAG * (carried[:, 3:6] - clump_vel[:, :, None] * carried[:, 6:7]) + STIFF * (
        clump_arm * pulled[:, 3:4] - pulled[:, 0:3]
    )
    load = jnp.concatenate(
        [jnp.sum(force, axis=2), jnp.sum(jnp.cross(clump_arm, force, axis=1), axis=2)], axis=1
    )
    return (fluid_density, load.T)


def solution(mesh):
    in_specs = (
        P("stream", "span", None, None),
        P("stream", "span", None, None),
        P("stream", "span", None),
        P("stream", "span"),
        P(AXES, None),
        P(AXES, None),
        P(AXES, None, None),
        P(AXES, None),
        P(AXES, None),
        P(AXES, None, None),
        P(AXES),
    )
    out_specs = (P("stream", "span", None), P(None, AXES))
    return jax.shard_map(body, mesh=mesh, in_specs=in_specs, out_specs=out_specs, check_vma=False)
```
